32 devices in a mesh: lat: 4 (over y, x), lon: 8 (over z, core).
Axes of the slice: x: 2, y: 2, z: 4, core: 2. Of those that a mesh axis runs over, the one named last changes fastest.
Arguments:
- air_mass: float32 [4, 32, 11520], P(None, 'lat', 'lon'), may hold values from 0.5 to 2
- tracer_mass: float32 [4, 4, 32, 11520], P(None, None, 'lat', 'lon'), may hold values from -6 to 6
- zonal_frac: float32 [4, 32, 11520], P(None, 'lat', 'lon'), may hold values from 0.05 to 0.95
- merid_courant: float32 [4, 32, 11520], P(None, 'lat', 'lon'), may hold values from -0.45 to 0.45
- zonal_shift: int32 [4, 32], P(None, 'lat'), may hold values from -5759 to 5759, as said below
Outputs:
- air_out: float32 [4, 32, 11520], P(None, 'lat', 'lon')
- tracer_out: float32 [4, 4, 32, 11520], P(None, None, 'lat', 'lon')
The draws below stay inside these ranges and needn't reach their ends.
Inputs may be any that keep to these rules, and one draw needn't show every extreme that they name: `zonal_shift`: row j lies (j + 1/2) / 5760 of a half circle from the pole; its whole-cell shifts may carry it across many longitude devices, in either direction.
All inputs are finite; a program needn't handle non-finite values.
Results may differ from the reference program's by a relative error of at most 0.0003.
Values sent between devices are 32-bit elements; how exact they have to be, the bound alone decides.
A program may use at most 64 MiB of HBM per device.

```python
import jax
import jax.numpy as jnp
from jax import lax

NLON = 11520
GLOBE_ROWS = 5760
TRACERS = 4
LEVELS = 4
ITERS = 2
NLAT = 32


def draw_zonal_shift(key, part):
    row_index = jnp.arange(NLAT, dtype=jnp.int32)
    largest = NLON // 2 - 1
    reach = (NLON // 64 + 1) * GLOBE_ROWS // 3
    bound = jnp.minimum(largest, reach // (2 * row_index + 1)).astype(jnp.int32)
    lower = jnp.broadcast_to(-bound[None, :], (LEVELS, NLAT))
    upper = jnp.broadcast_to(bound[None, :] + 1, (LEVELS, NLAT))
    values = jax.random.randint(key, (LEVELS, NLAT), lower, upper, dtype=jnp.int32)
    values = values.at[0, 0].set(largest)
    values = values.at[1, 0].set(-largest)
    return values


def block_scale(stream_key, extent, shards, least, top_value):
    def one(dim, blocks):
        steps = jax.random.uniform(jax.random.fold_in(jax.random.fold_in(stream_key, 6), dim), (blocks,), jnp.float32, least / len(shards), top_value / len(shards))
        return jnp.repeat(jnp.exp(steps), extent[dim] // blocks).reshape((-1,) + (1,) * (len(extent) - dim - 1))

    factor_of = one(*shards[0])
    for cut in shards[1:]:
        factor_of = factor_of * one(*cut)
    return factor_of


def gaussian(rng, extent, deviation, limit, pieces=(), kind=jnp.bfloat16):
    values = deviation * jax.random.normal(rng, extent, jnp.float32)
    if pieces:
        values = values * block_scale(rng, extent, pieces, -0.22, 0.18)
    return jnp.clip(values, -limit, limit).astype(kind)


def setup_inputs(seed: int = 0) -> dict:
    key_of = jax.random.split(jax.random.key(seed), 6)
    return {
        "air_mass": jnp.clip(0.5 + 1.5 * jax.random.uniform(key_of[0], (LEVELS, NLAT, NLON), jnp.float32) ** block_scale(key_of[0], (LEVELS, NLAT, NLON), ((1, 4), (2, 8)), -0.2, 0.2), 0.5, 2.0),
        "tracer_mass": gaussian(key_of[1], (TRACERS, LEVELS, NLAT, NLON), 1.0, 6.0, ((2, 4), (3, 8)), jnp.float32),
        "zonal_frac": jnp.clip(0.05 + 0.9 * jax.random.uniform(key_of[2], (LEVELS, NLAT, NLON), jnp.float32) ** block_scale(key_of[2], (LEVELS, NLAT, NLON), ((1, 4), (2, 8)), -0.2, 0.2), 0.05, 0.95),
        "merid_courant": jnp.clip(jax.random.uniform(key_of[3], (LEVELS, NLAT, NLON), jnp.float32, -0.45, 0.45) * block_scale(key_of[3], (LEVELS, NLAT, NLON), ((1, 4), (2, 8)), -0.4, 0.0), -0.45, 0.45),
        "zonal_shift": draw_zonal_shift(jax.random.fold_in(key_of[5], 71), 0),
    }


def right_amount(centre, left_edge, right_edge, fraction):
    slope = right_edge - left_edge
    curve = 6.0 * centre - 3.0 * (left_edge + right_edge)
    return fraction * (right_edge - 0.5 * fraction * (slope - (1.0 - fraction * (2.0 / 3.0)) * curve))


def left_amount(centre, left_edge, right_edge, fraction):
    slope = right_edge - left_edge
    curve = 6.0 * centre - 3.0 * (left_edge + right_edge)
    return fraction * (left_edge + 0.5 * fraction * (slope + (1.0 - fraction * (2.0 / 3.0)) * curve))


def zonal_update(padded, padded_frac):
    faces = (7.0 * (padded[..., 1:-2] + padded[..., 2:-1]) - (padded[..., :-3] + padded[..., 3:])) / 12.0
    cells = padded.shape[-1] - 6
    fluxes = right_amount(padded[..., 2:cells + 3], faces[..., 0:cells + 1], faces[..., 1:cells + 2], padded_frac[..., 3:cells + 4])
    return padded[..., 3:cells + 3] + fluxes[..., :cells] - fluxes[..., 1:]


def merid_update(padded, padded_courant):
    faces = (7.0 * (padded[..., 1:-2, :] + padded[..., 2:-1, :]) - (padded[..., :-3, :] + padded[..., 3:, :])) / 12.0
    cells = padded.shape[-2] - 6
    courant = padded_courant[..., 3:cells + 4, :]
    northward = jnp.maximum(courant, 0.0)
    southward = jnp.maximum(-courant, 0.0)
    fluxes = right_amount(padded[..., 2:cells + 3, :], faces[..., 0:cells + 1, :], faces[..., 1:cells + 2, :], northward)
    fluxes = fluxes - left_amount(padded[..., 3:cells + 4, :], faces[..., 1:cells + 2, :], faces[..., 2:cells + 3, :], southward)
    return padded[..., 3:cells + 3, :] + fluxes[..., :cells, :] - fluxes[..., 1:, :]


def level_step(inputs):
    fields, frac, courant, shifts = inputs
    row_index = jnp.arange(NLAT, dtype=jnp.int32)[:, None]
    courant = jnp.where(row_index == 0, jnp.zeros_like(courant), courant)
    source_index = jnp.mod(jnp.arange(NLON, dtype=jnp.int32)[None, :] - shifts[:, None], NLON).astype(jnp.int32)
    source_index = jnp.broadcast_to(source_index[None], fields.shape)
    padded_frac = jnp.concatenate([frac[:, -3:], frac, frac[:, :3]], axis=1)
    padded_courant = jnp.pad(courant, ((3, 3), (0, 0)))
    for step in range(ITERS):
        moved = jnp.take_along_axis(fields, source_index, axis=2)
        padded = jnp.concatenate([moved[..., -3:], moved, moved[..., :3]], axis=2)
        fields = zonal_update(padded, padded_frac)
        padded = jnp.pad(fields, ((0, 0), (3, 3), (0, 0)))
        fields = merid_update(padded, padded_courant)
    return fields


def reference(air_mass, tracer_mass, zonal_frac, merid_courant, zonal_shift):
    fields = jnp.concatenate([air_mass[None], tracer_mass], axis=0)
    by_level = jnp.moveaxis(fields, 1, 0)
    result = lax.map(level_step, (by_level, zonal_frac, merid_courant, zonal_shift))
    result = jnp.moveaxis(result, 0, 1)
    return result[0], result[1:]
```

```python
import functools

import jax
import jax.numpy as jnp
from jax import lax
from jax.experimental import pallas as pl
from jax.experimental.pallas import tpu as pltpu
from jax.sharding import PartitionSpec as P

ITERS = 2
HALO = 3
LANES = 128


def round_up(value, unit=LANES):
    return -(-value // unit) * unit


def exchange(array, stride):
    count = lax.axis_size("lon")
    return lax.ppermute(array, "lon", [(i, i ^ stride) for i in range(count)])


def lat_halos(block, dim):
    count = lax.axis_size("lat")
    forward = [(i, i + 1) for i in range(count - 1)]
    backward = [(b, a) for a, b in forward]
    size = block.shape[dim]
    south = lax.ppermute(lax.slice_in_dim(block, size - HALO, size, axis=dim), "lat", forward)
    north = lax.ppermute(lax.slice_in_dim(block, 0, HALO, axis=dim), "lat", backward)
    return south, north


def right_amount(centre, left_edge, right_edge, fraction):
    slope = right_edge - left_edge
    curve = 6.0 * centre - 3.0 * (left_edge + right_edge)
    return fraction * (
        right_edge - 0.5 * fraction * (slope - (1.0 - fraction * (2.0 / 3.0)) * curve)
    )


def left_amount(centre, left_edge, right_edge, fraction):
    slope = right_edge - left_edge
    curve = 6.0 * centre - 3.0 * (left_edge + right_edge)
    return fraction * (
        left_edge + 0.5 * fraction * (slope + (1.0 - fraction * (2.0 / 3.0)) * curve)
    )


def window_kernel(held, lead, width, plan, *refs):
    own = refs[:held]
    other = refs[held : 2 * held]
    mine, theirs, joined = refs[2 * held :]
    comps, band, _ = mine.shape
    out_width = mine.shape[2]

    def fill(low, high):
        for t in range(held):
            joined[t, :, :, lead : lead + width] = low[t][...]
            joined[t, :, :, lead + width : lead + 2 * width] = high[t][...]

    core = plan[0, 0]

    @pl.when(core == 0)
    def _():
        fill(own, other)

    @pl.when(core != 0)
    def _():
        fill(other, own)

    lane = lax.broadcasted_iota(jnp.int32, (comps, 1, LANES), 2)
    for target, out in ((1, mine), (3, theirs)):
        for j in range(band):
            slot = plan[target, j]
            first = plan[target + 1, j]
            begin = lead + jnp.maximum(first, -lead)
            tile = begin // LANES
            rest = begin - tile * LANES
            back = jnp.where(rest == 0, 0, LANES - rest)

            def piece(m):
                values = joined[slot, :, j : j + 1, pl.ds(pl.multiple_of((tile + m) * LANES, LANES), LANES)]
                return pltpu.roll(values, back, 2)

            now = piece(0)
            for m in range(out_width // LANES):
                later = piece(m + 1)
                values = jnp.where(lane < LANES - rest, now, later)
                place = lane + (first + m * LANES)
                inside = (place >= 0) & (place < 2 * width)
                out[:, j : j + 1, m * LANES : (m + 1) * LANES] = jnp.where(inside, values, 0.0)
                now = later


def cut_windows(own, other, plan):
    held = len(own)
    comps, band, width = own[0].shape
    out_width = round_up(width + 2 * HALO)
    lead = out_width
    total = round_up(lead + 2 * width) + out_width + 2 * LANES
    shape = jax.ShapeDtypeStruct((comps, band, out_width), jnp.float32)
    return pl.pallas_call(
        functools.partial(window_kernel, held, lead, width),
        out_shape=(shape, shape),
        in_specs=[pl.BlockSpec(memory_space=pltpu.SMEM)]
        + [pl.BlockSpec(memory_space=pltpu.VMEM)] * (2 * held),
        out_specs=(pl.BlockSpec(memory_space=pltpu.VMEM),) * 2,
        scratch_shapes=[pltpu.VMEM((held, comps, band, total), jnp.float32)],
        compiler_params=pltpu.CompilerParams(vmem_limit_bytes=32 * 1024 * 1024),
        cost_estimate=pl.CostEstimate(flops=2_000_000, bytes_accessed=2_000_000, transcendentals=0),
        name="cut_windows",
    )(plan, *own, *other)


def zonal_kernel(mine, theirs, frac, out):
    comps, band, width = out.shape
    full = mine.shape[2]
    fraction = frac[...]
    for c in range(comps):
        w = mine[c] + theirs[c]
        w_1 = pltpu.roll(w, 1, 1)
        w_2 = pltpu.roll(w, 2, 1)
        w1 = pltpu.roll(w, full - 1, 1)
        face = (7.0 * (w_1 + w) - (w_2 + w1)) / 12.0
        flux = right_amount(w_1, pltpu.roll(face, 1, 1), face, fraction)
        new = w + flux - pltpu.roll(flux, full - 1, 1)
        out[c] = pltpu.roll(new, full - HALO, 1)[:, :width]


def zonal(mine, theirs, frac, width):
    comps, band, _ = mine.shape
    return pl.pallas_call(
        zonal_kernel,
        out_shape=jax.ShapeDtypeStruct((comps, band, width), jnp.float32),
        cost_estimate=pl.CostEstimate(flops=2_000_000, bytes_accessed=1_000_000, transcendentals=0),
        name="zonal",
    )(mine, theirs, frac)


def merid_kernel(fields, south, north, courant, out):
    comps, band, width = out.shape
    step = 2 * LANES
    for at in range(0, width, step):
        cols = slice(at, min(at + step, width))
        g = courant[HALO : HALO + band + 1, cols]
        northward = jnp.maximum(g, 0.0)
        southward = jnp.maximum(-g, 0.0)
        for c in range(comps):
            padded = jnp.concatenate([south[c, :, cols], fields[c, :, cols], north[c, :, cols]], axis=0)
            faces = (7.0 * (padded[1:-2] + padded[2:-1]) - (padded[:-3] + padded[3:])) / 12.0
            flux = right_amount(
                padded[2 : band + 3], faces[0 : band + 1], faces[1 : band + 2], northward
            ) - left_amount(
                padded[3 : band + 4], faces[1 : band + 2], faces[2 : band + 3], southward
            )
            out[c, :, cols] = padded[3 : band + 3] + flux[:band] - flux[1:]


def merid(fields, south, north, courant):
    return pl.pallas_call(
        merid_kernel,
        out_shape=jax.ShapeDtypeStruct(fields.shape, jnp.float32),
        cost_estimate=pl.CostEstimate(flops=4_000_000, bytes_accessed=1_000_000, transcendentals=0),
        name="merid",
    )(fields, south, north, courant)


def make_plan(shift, width, count, me):
    full = width * count
    parity = me // 2 % 2

    def towards(device):
        begin = jnp.mod(device * width - HALO - shift, full)
        pair = begin // (2 * width)
        offset = begin - pair * (2 * width)
        here = pair % 2 == parity
        chosen = jnp.where(here, pair, (pair + 1) % (count // 2))
        slot = (chosen // 2) ^ (me // 4)
        return [slot, jnp.where(here, offset, offset - 2 * width)]

    core = jnp.broadcast_to(me % 2, shift.shape)
    rows = [core] + towards(me) + towards(me ^ 2)
    return jnp.stack(rows, axis=1).astype(jnp.int32)


def local(air_mass, tracer_mass, zonal_frac, merid_courant, zonal_shift):
    levels, band, width = air_mass.shape
    count = lax.axis_size("lon")
    me = lax.axis_index("lon")
    global_row = lax.axis_index("lat") * band + jnp.arange(band, dtype=jnp.int32)
    courant = jnp.where(
        global_row[None, :, None] == 0, jnp.zeros_like(merid_courant), merid_courant
    )
    plan = make_plan(zonal_shift, width, count, me)

    ring = [(i, (i + 1) % count) for i in range(count)]
    west = lax.ppermute(zonal_frac[..., width - HALO :], "lon", ring)
    east = lax.ppermute(zonal_frac[..., :HALO], "lon", [(b, a) for a, b in ring])
    out_width = round_up(width + 2 * HALO)
    fill = jnp.zeros((levels, band, out_width - width - 2 * HALO), jnp.float32)
    frac = jnp.concatenate([west, zonal_frac, east, fill], axis=2)
    south, north = lat_halos(courant, 1)
    courant = jnp.concatenate([south, courant, north], axis=1)

    fields = [
        jnp.concatenate([air_mass[None, l], tracer_mass[:, l]], axis=0) for l in range(levels)
    ]
    for step in range(ITERS):
        held = [[f] for f in fields]
        stride = 4
        while stride < count:
            for l in range(levels):
                held[l] = held[l] + [exchange(x, stride) for x in held[l]]
            stride *= 2
        for l in range(levels):
            other = [exchange(x, 1) for x in held[l]]
            mine, theirs = cut_windows(held[l], other, plan[l])
            theirs = exchange(theirs, 2)
            moved = zonal(mine, theirs, frac[l], width)
            south, north = lat_halos(moved, 1)
            fields[l] = merid(moved, south, north, courant[l])
    result = jnp.stack(fields, axis=1)
    return (result[0], result[1:])


def solution(mesh):
    return jax.shard_map(
        local,
        mesh=mesh,
        in_specs=(
            P(None, "lat", "lon"),
            P(None, None, "lat", "lon"),
            P(None, "lat", "lon"),
            P(None, "lat", "lon"),
            P(None, "lat"),
        ),
        out_specs=(P(None, "lat", "lon"), P(None, None, "lat", "lon")),
        check_vma=False,
    )
```

```python
import functools

import jax
import jax.numpy as jnp
from jax import lax
from jax.experimental import pallas as pl
from jax.experimental.pallas import tpu as pltpu
from jax.sharding import PartitionSpec as P

ITERS = 2
HALO = 3
LANES = 128


def round_up(value, unit=LANES):
    return -(-value // unit) * unit


def exchange(array, stride):
    count = lax.axis_size("lon")
    return lax.ppermute(array, "lon", [(i, i ^ stride) for i in range(count)])


def lat_halos(block, dim):
    count = lax.axis_size("lat")
    forward = [(i, i + 1) for i in range(count - 1)]
    backward = [(b, a) for a, b in forward]
    size = block.shape[dim]
    south = lax.ppermute(lax.slice_in_dim(block, size - HALO, size, axis=dim), "lat", forward)
    north = lax.ppermute(lax.slice_in_dim(block, 0, HALO, axis=dim), "lat", backward)
    return south, north


def right_amount(centre, left_edge, right_edge, fraction):
    slope = right_edge - left_edge
    curve = 6.0 * centre - 3.0 * (left_edge + right_edge)
    return fraction * (
        right_edge - 0.5 * fraction * (slope - (1.0 - fraction * (2.0 / 3.0)) * curve)
    )


def left_amount(centre, left_edge, right_edge, fraction):
    slope = right_edge - left_edge
    curve = 6.0 * centre - 3.0 * (left_edge + right_edge)
    return fraction * (
        left_edge + 0.5 * fraction * (slope + (1.0 - fraction * (2.0 / 3.0)) * curve)
    )


def window_kernel(held, lead, width, plan, *refs):
    own = refs[:held]
    other = refs[held : 2 * held]
    mine, theirs, joined = refs[2 * held :]
    comps, band, _ = mine.shape
    out_width = mine.shape[2]

    def fill(low, high):
        for t in range(held):
            joined[t, :, :, lead : lead + width] = low[t][...]
            joined[t, :, :, lead + width : lead + 2 * width] = high[t][...]

    core = plan[0, 0]

    @pl.when(core == 0)
    def _():
        fill(own, other)

    @pl.when(core != 0)
    def _():
        fill(other, own)

    lane = lax.broadcasted_iota(jnp.int32, (comps, 1, LANES), 2)
    for target, out in ((1, mine), (3, theirs)):
        for j in range(band):
            slot = plan[target, j]
            first = plan[target + 1, j]
            begin = lead + jnp.maximum(first, -lead)
            tile = begin // LANES
            rest = begin - tile * LANES
            back = jnp.where(rest == 0, 0, LANES - rest)

            def piece(m):
                values = joined[slot, :, j : j + 1, pl.ds(pl.multiple_of((tile + m) * LANES, LANES), LANES)]
                return pltpu.roll(values, back, 2)

            now = piece(0)
            for m in range(out_width // LANES):
                later = piece(m + 1)
                values = jnp.where(lane < LANES - rest, now, later)
                place = lane + (first + m * LANES)
                inside = (place >= 0) & (place < 2 * width)
                out[:, j : j + 1, m * LANES : (m + 1) * LANES] = jnp.where(inside, values, 0.0)
                now = later


def cut_windows(own, other, plan):
    held = len(own)
    comps, band, width = own[0].shape
    out_width = round_up(width + 2 * HALO)
    lead = out_width
    total = round_up(lead + 2 * width) + out_width + 2 * LANES
    shape = jax.ShapeDtypeStruct((comps, band, out_width), jnp.float32)
    return pl.pallas_call(
        functools.partial(window_kernel, held, lead, width),
        out_shape=(shape, shape),
        in_specs=[pl.BlockSpec(memory_space=pltpu.SMEM)]
        + [pl.BlockSpec(memory_space=pltpu.VMEM)] * (2 * held),
        out_specs=(pl.BlockSpec(memory_space=pltpu.VMEM),) * 2,
        scratch_shapes=[pltpu.VMEM((held, comps, band, total), jnp.float32)],
        compiler_params=pltpu.CompilerParams(vmem_limit_bytes=32 * 1024 * 1024),
        cost_estimate=pl.CostEstimate(flops=2_000_000, bytes_accessed=2_000_000, transcendentals=0),
        name="cut_windows",
    )(plan, *own, *other)


def stencil_kernel(levels, rows, *refs):
    mine = refs[:levels]
    theirs = refs[levels : 2 * levels]
    frac, courant = refs[2 * levels : 2 * levels + 2]
    out = refs[2 * levels + 2 : 3 * levels + 2]
    to_north, to_south, south, north, send_sem, recv_sem = refs[3 * levels + 2 :]
    comps, band, width = out[0].shape
    full = mine[0].shape[2]
    count = lax.axis_size("lat")
    me = lax.axis_index("lat")
    has_south = me > 0
    has_north = me < count - 1
    used = comps * HALO

    barrier = pltpu.get_barrier_semaphore()

    def greet(step):
        pl.semaphore_signal(
            barrier, inc=1, device_id={"lat": me + step}, device_id_type=pl.DeviceIdType.MESH
        )

    pl.when(has_south)(lambda: greet(-1))
    pl.when(has_north)(lambda: greet(1))

    def northward_copy(l):
        return pltpu.make_async_remote_copy(
            src_ref=to_north.at[l], dst_ref=south.at[l],
            send_sem=send_sem.at[0, l], recv_sem=recv_sem.at[0, l],
            device_id={"lat": me + 1}, device_id_type=pl.DeviceIdType.MESH,
        )

    def southward_copy(l):
        return pltpu.make_async_remote_copy(
            src_ref=to_south.at[l], dst_ref=north.at[l],
            send_sem=send_sem.at[1, l], recv_sem=recv_sem.at[1, l],
            device_id={"lat": me - 1}, device_id_type=pl.DeviceIdType.MESH,
        )

    @pl.when(me == 0)
    def _():
        south[...] = jnp.zeros_like(south)

    @pl.when(me == count - 1)
    def _():
        north[...] = jnp.zeros_like(north)

    for l in range(levels):
        fraction = frac[l]
        for c in range(comps):
            w = mine[l][c] + theirs[l][c]
            w_1 = pltpu.roll(w, 1, 1)
            w_2 = pltpu.roll(w, 2, 1)
            w1 = pltpu.roll(w, full - 1, 1)
            face = (7.0 * (w_1 + w) - (w_2 + w1)) * (1.0 / 12.0)
            flux = right_amount(w_1, pltpu.roll(face, 1, 1), face, fraction)
            new = w + flux - pltpu.roll(flux, full - 1, 1)
            new = pltpu.roll(new, full - HALO, 1)[:, :width]
            out[l][c] = new
            to_north[l, c * HALO : (c + 1) * HALO] = new[band - HALO :]
            to_south[l, c * HALO : (c + 1) * HALO] = new[:HALO]
        if rows > used:
            pad = jnp.zeros((rows - used, width), jnp.float32)
            to_north[l, used:rows] = pad
            to_south[l, used:rows] = pad
        if l == 0:
            peers = has_south.astype(jnp.int32) + has_north.astype(jnp.int32)
            pl.semaphore_wait(barrier, peers)
        pl.when(has_north)(lambda l=l: northward_copy(l).start())
        pl.when(has_south)(lambda l=l: southward_copy(l).start())

    step = 2 * LANES
    for l in range(levels):
        pl.when(has_south)(lambda l=l: northward_copy(l).wait_recv())
        pl.when(has_north)(lambda l=l: southward_copy(l).wait_recv())
        for at in range(0, width, step):
            cols = slice(at, min(at + step, width))
            g = courant[l, HALO : HALO + band + 1, cols]
            northward = jnp.maximum(g, 0.0)
            southward = jnp.maximum(-g, 0.0)
            for c in range(comps):
                ends = slice(c * HALO, (c + 1) * HALO)
                padded = jnp.concatenate(
                    [south[l, ends, cols], out[l][c, :, cols], north[l, ends, cols]], axis=0
                )
                faces = (
                    7.0 * (padded[1:-2] + padded[2:-1]) - (padded[:-3] + padded[3:])
                ) * (1.0 / 12.0)
                flux = right_amount(
                    padded[2 : band + 3], faces[0 : band + 1], faces[1 : band + 2], northward
                ) - left_amount(
                    padded[3 : band + 4], faces[1 : band + 2], faces[2 : band + 3], southward
                )
                out[l][c, :, cols] = padded[3 : band + 3] + flux[:band] - flux[1:]

    for l in range(levels):
        pl.when(has_north)(lambda l=l: northward_copy(l).wait_send())
        pl.when(has_south)(lambda l=l: southward_copy(l).wait_send())


def stencils(mine, theirs, frac, courant, width, step):
    levels = len(mine)
    comps, band, _ = mine[0].shape
    rows = round_up(comps * HALO, 8)
    shape = jax.ShapeDtypeStruct((comps, band, width), jnp.float32)
    vmem = pl.BlockSpec(memory_space=pltpu.VMEM)
    halo = pltpu.VMEM((levels, rows, width), jnp.float32)
    return pl.pallas_call(
        functools.partial(stencil_kernel, levels, rows),
        out_shape=(shape,) * levels,
        in_specs=[vmem] * (2 * levels + 2),
        out_specs=(vmem,) * levels,
        scratch_shapes=[
            halo, halo, halo, halo,
            pltpu.SemaphoreType.DMA((2, levels)),
            pltpu.SemaphoreType.DMA((2, levels)),
        ],
        compiler_params=pltpu.CompilerParams(
            vmem_limit_bytes=32 * 1024 * 1024, collective_id=step, has_side_effects=True
        ),
        cost_estimate=pl.CostEstimate(flops=20_000_000, bytes_accessed=5_000_000, transcendentals=0),
        name="stencils",
    )(*mine, *theirs, frac, courant)


def make_plan(shift, width, count, me):
    full = width * count
    parity = me // 2 % 2

    def towards(device):
        begin = jnp.mod(device * width - HALO - shift, full)
        pair = begin // (2 * width)
        offset = begin - pair * (2 * width)
        here = pair % 2 == parity
        chosen = jnp.where(here, pair, (pair + 1) % (count // 2))
        slot = (chosen // 2) ^ (me // 4)
        return [slot, jnp.where(here, offset, offset - 2 * width)]

    core = jnp.broadcast_to(me % 2, shift.shape)
    rows = [core] + towards(me) + towards(me ^ 2)
    return jnp.stack(rows, axis=1).astype(jnp.int32)


def local(air_mass, tracer_mass, zonal_frac, merid_courant, zonal_shift):
    levels, band, width = air_mass.shape
    count = lax.axis_size("lon")
    me = lax.axis_index("lon")
    global_row = lax.axis_index("lat") * band + jnp.arange(band, dtype=jnp.int32)
    courant = jnp.where(
        global_row[None, :, None] == 0, jnp.zeros_like(merid_courant), merid_courant
    )
    plan = make_plan(zonal_shift, width, count, me)

    ring = [(i, (i + 1) % count) for i in range(count)]
    west = lax.ppermute(zonal_frac[..., width - HALO :], "lon", ring)
    east = lax.ppermute(zonal_frac[..., :HALO], "lon", [(b, a) for a, b in ring])
    out_width = round_up(width + 2 * HALO)
    fill = jnp.zeros((levels, band, out_width - width - 2 * HALO), jnp.float32)
    frac = jnp.concatenate([west, zonal_frac, east, fill], axis=2)
    south, north = lat_halos(courant, 1)
    courant = jnp.concatenate([south, courant, north], axis=1)

    fields = [
        jnp.concatenate([air_mass[None, l], tracer_mass[:, l]], axis=0) for l in range(levels)
    ]
    for step in range(ITERS):
        held = [[f] for f in fields]
        stride = 4
        while stride < count:
            for l in range(levels):
                held[l] = held[l] + [exchange(x, stride) for x in held[l]]
            stride *= 2
        mine, theirs = [], []
        for l in range(levels):
            other = [exchange(x, 1) for x in held[l]]
            kept, sent = cut_windows(held[l], other, plan[l])
            mine.append(kept)
            theirs.append(exchange(sent, 2))
        fields = stencils(mine, theirs, frac, courant, width, step)
    result = jnp.stack(fields, axis=1)
    return (result[0], result[1:])


def solution(mesh):
    return jax.shard_map(
        local,
        mesh=mesh,
        in_specs=(
            P(None, "lat", "lon"),
            P(None, None, "lat", "lon"),
            P(None, "lat", "lon"),
            P(None, "lat", "lon"),
            P(None, "lat"),
        ),
        out_specs=(P(None, "lat", "lon"), P(None, None, "lat", "lon")),
        check_vma=False,
    )
```

```python
import functools

import jax
import jax.numpy as jnp
from jax import lax
from jax.experimental import pallas as pl
from jax.experimental.pallas import tpu as pltpu
from jax.sharding import PartitionSpec as P

ITERS = 2
HALO = 3
LANES = 128


def round_up(value, unit=LANES):
    return -(-value // unit) * unit


def exchange(array, stride):
    count = lax.axis_size("lon")
    return lax.ppermute(array, "lon", [(i, i ^ stride) for i in range(count)])


def lat_halos(block, dim):
    count = lax.axis_size("lat")
    forward = [(i, i + 1) for i in range(count - 1)]
    backward = [(b, a) for a, b in forward]
    size = block.shape[dim]
    south = lax.ppermute(lax.slice_in_dim(block, size - HALO, size, axis=dim), "lat", forward)
    north = lax.ppermute(lax.slice_in_dim(block, 0, HALO, axis=dim), "lat", backward)
    return south, north


def right_amount(centre, left_edge, right_edge, fraction):
    slope = right_edge - left_edge
    curve = 6.0 * centre - 3.0 * (left_edge + right_edge)
    return fraction * (
        right_edge - 0.5 * fraction * (slope - (1.0 - fraction * (2.0 / 3.0)) * curve)
    )


def window_kernel(held, lead, width, plan, *refs):
    own = refs[:held]
    other = refs[held : 2 * held]
    mine, theirs, joined = refs[2 * held :]
    comps, band, _ = mine.shape
    out_width = mine.shape[2]

    def fill(low, high):
        for t in range(held):
            joined[t, :, :, lead : lead + width] = low[t][...]
            joined[t, :, :, lead + width : lead + 2 * width] = high[t][...]

    core = plan[0, 0]

    @pl.when(core == 0)
    def _():
        fill(own, other)

    @pl.when(core != 0)
    def _():
        fill(other, own)

    lane = lax.broadcasted_iota(jnp.int32, (comps, 1, LANES), 2)
    for target, out in ((1, mine), (3, theirs)):
        for j in range(band):
            slot = plan[target, j]
            first = plan[target + 1, j]
            begin = lead + jnp.maximum(first, -lead)
            tile = begin // LANES
            rest = begin - tile * LANES
            back = jnp.where(rest == 0, 0, LANES - rest)

            def piece(m):
                values = joined[slot, :, j : j + 1, pl.ds(pl.multiple_of((tile + m) * LANES, LANES), LANES)]
                return pltpu.roll(values, back, 2)

            now = piece(0)
            for m in range(out_width // LANES):
                later = piece(m + 1)
                values = jnp.where(lane < LANES - rest, now, later)
                place = lane + (first + m * LANES)
                inside = (place >= 0) & (place < 2 * width)
                out[:, j : j + 1, m * LANES : (m + 1) * LANES] = jnp.where(inside, values, 0.0)
                now = later


def cut_windows(own, other, plan):
    held = len(own)
    comps, band, width = own[0].shape
    out_width = round_up(width + 2 * HALO)
    lead = out_width
    total = round_up(lead + 2 * width) + out_width + 2 * LANES
    shape = jax.ShapeDtypeStruct((comps, band, out_width), jnp.float32)
    return pl.pallas_call(
        functools.partial(window_kernel, held, lead, width),
        out_shape=(shape, shape),
        in_specs=[pl.BlockSpec(memory_space=pltpu.SMEM)]
        + [pl.BlockSpec(memory_space=pltpu.VMEM)] * (2 * held),
        out_specs=(pl.BlockSpec(memory_space=pltpu.VMEM),) * 2,
        scratch_shapes=[pltpu.VMEM((held, comps, band, total), jnp.float32)],
        compiler_params=pltpu.CompilerParams(vmem_limit_bytes=32 * 1024 * 1024),
        cost_estimate=pl.CostEstimate(flops=2_000_000, bytes_accessed=2_000_000, transcendentals=0),
        name="cut_windows",
    )(plan, *own, *other)


def stencil_kernel(levels, rows, *refs):
    mine = refs[:levels]
    theirs = refs[levels : 2 * levels]
    frac, courant = refs[2 * levels : 2 * levels + 2]
    out = refs[2 * levels + 2 : 3 * levels + 2]
    to_north, to_south, south, north, send_sem, recv_sem = refs[3 * levels + 2 :]
    comps, band, width = out[0].shape
    full = mine[0].shape[2]
    count = lax.axis_size("lat")
    me = lax.axis_index("lat")
    has_south = me > 0
    has_north = me < count - 1
    used = comps * HALO

    barrier = pltpu.get_barrier_semaphore()

    def greet(step):
        pl.semaphore_signal(
            barrier, inc=1, device_id={"lat": me + step}, device_id_type=pl.DeviceIdType.MESH
        )

    pl.when(has_south)(lambda: greet(-1))
    pl.when(has_north)(lambda: greet(1))

    def northward_copy(l):
        return pltpu.make_async_remote_copy(
            src_ref=to_north.at[l], dst_ref=south.at[l],
            send_sem=send_sem.at[0, l], recv_sem=recv_sem.at[0, l],
            device_id={"lat": me + 1}, device_id_type=pl.DeviceIdType.MESH,
        )

    def southward_copy(l):
        return pltpu.make_async_remote_copy(
            src_ref=to_south.at[l], dst_ref=north.at[l],
            send_sem=send_sem.at[1, l], recv_sem=recv_sem.at[1, l],
            device_id={"lat": me - 1}, device_id_type=pl.DeviceIdType.MESH,
        )

    @pl.when(me == 0)
    def _():
        south[...] = jnp.zeros_like(south)

    @pl.when(me == count - 1)
    def _():
        north[...] = jnp.zeros_like(north)

    for l in range(levels):
        fraction = frac[l]
        for c in range(comps):
            w = mine[l][c] + theirs[l][c]
            w_1 = pltpu.roll(w, 1, 1)
            w_2 = pltpu.roll(w, 2, 1)
            w1 = pltpu.roll(w, full - 1, 1)
            face = (7.0 * (w_1 + w) - (w_2 + w1)) * (1.0 / 12.0)
            flux = right_amount(w_1, pltpu.roll(face, 1, 1), face, fraction)
            new = w + flux - pltpu.roll(flux, full - 1, 1)
            new = pltpu.roll(new, full - HALO, 1)[:, :width]
            out[l][c] = new
            to_north[l, c * HALO : (c + 1) * HALO] = new[band - HALO :]
            to_south[l, c * HALO : (c + 1) * HALO] = new[:HALO]
        if rows > used:
            pad = jnp.zeros((rows - used, width), jnp.float32)
            to_north[l, used:rows] = pad
            to_south[l, used:rows] = pad
        if l == 0:
            peers = has_south.astype(jnp.int32) + has_north.astype(jnp.int32)
            pl.semaphore_wait(barrier, peers)
        pl.when(has_north)(lambda l=l: northward_copy(l).start())
        pl.when(has_south)(lambda l=l: southward_copy(l).start())

    step = 2 * LANES
    for l in range(levels):
        pl.when(has_south)(lambda l=l: northward_copy(l).wait_recv())
        pl.when(has_north)(lambda l=l: southward_copy(l).wait_recv())
        for at in range(0, width, step):
            cols = slice(at, min(at + step, width))
            g = courant[l, HALO : HALO + band + 1, cols]
            half = 0.5 * g * g
            rest = 1.0 - jnp.abs(g) * (2.0 / 3.0)
            north_going = g > 0.0
            rest = jnp.where(north_going, rest, -rest)
            for c in range(comps):
                ends = slice(c * HALO, (c + 1) * HALO)
                padded = jnp.concatenate(
                    [south[l, ends, cols], out[l][c, :, cols], north[l, ends, cols]], axis=0
                )
                faces = (
                    7.0 * (padded[1:-2] + padded[2:-1]) - (padded[:-3] + padded[3:])
                ) * (1.0 / 12.0)
                slope = faces[1:] - faces[:-1]
                curve = 6.0 * padded[2 : band + 4] - 3.0 * (faces[1:] + faces[:-1])
                slope = jnp.where(north_going, slope[:-1], slope[1:])
                curve = jnp.where(north_going, curve[:-1], curve[1:])
                flux = g * faces[1 : band + 2] - half * (slope - rest * curve)
                out[l][c, :, cols] = padded[3 : band + 3] + flux[:band] - flux[1:]

    for l in range(levels):
        pl.when(has_north)(lambda l=l: northward_copy(l).wait_send())
        pl.when(has_south)(lambda l=l: southward_copy(l).wait_send())


def stencils(mine, theirs, frac, courant, width, step):
    levels = len(mine)
    comps, band, _ = mine[0].shape
    rows = round_up(comps * HALO, 8)
    shape = jax.ShapeDtypeStruct((comps, band, width), jnp.float32)
    vmem = pl.BlockSpec(memory_space=pltpu.VMEM)
    halo = pltpu.VMEM((levels, rows, width), jnp.float32)
    return pl.pallas_call(
        functools.partial(stencil_kernel, levels, rows),
        out_shape=(shape,) * levels,
        in_specs=[vmem] * (2 * levels + 2),
        out_specs=(vmem,) * levels,
        scratch_shapes=[
            halo, halo, halo, halo,
            pltpu.SemaphoreType.DMA((2, levels)),
            pltpu.SemaphoreType.DMA((2, levels)),
        ],
        compiler_params=pltpu.CompilerParams(
            vmem_limit_bytes=32 * 1024 * 1024, collective_id=step, has_side_effects=True
        ),
        cost_estimate=pl.CostEstimate(flops=20_000_000, bytes_accessed=5_000_000, transcendentals=0),
        name="stencils",
    )(*mine, *theirs, frac, courant)


def make_plan(shift, width, count, me):
    full = width * count
    parity = me // 2 % 2

    def towards(device):
        begin = jnp.mod(device * width - HALO - shift, full)
        pair = begin // (2 * width)
        offset = begin - pair * (2 * width)
        here = pair % 2 == parity
        chosen = jnp.where(here, pair, (pair + 1) % (count // 2))
        slot = (chosen // 2) ^ (me // 4)
        return [slot, jnp.where(here, offset, offset - 2 * width)]

    core = jnp.broadcast_to(me % 2, shift.shape)
    rows = [core] + towards(me) + towards(me ^ 2)
    return jnp.stack(rows, axis=1).astype(jnp.int32)


def local(air_mass, tracer_mass, zonal_frac, merid_courant, zonal_shift):
    levels, band, width = air_mass.shape
    count = lax.axis_size("lon")
    me = lax.axis_index("lon")
    global_row = lax.axis_index("lat") * band + jnp.arange(band, dtype=jnp.int32)
    courant = jnp.where(
        global_row[None, :, None] == 0, jnp.zeros_like(merid_courant), merid_courant
    )
    plan = make_plan(zonal_shift, width, count, me)

    ring = [(i, (i + 1) % count) for i in range(count)]
    west = lax.ppermute(zonal_frac[..., width - HALO :], "lon", ring)
    east = lax.ppermute(zonal_frac[..., :HALO], "lon", [(b, a) for a, b in ring])
    out_width = round_up(width + 2 * HALO)
    fill = jnp.zeros((levels, band, out_width - width - 2 * HALO), jnp.float32)
    frac = jnp.concatenate([west, zonal_frac, east, fill], axis=2)
    south, north = lat_halos(courant, 1)
    courant = jnp.concatenate([south, courant, north], axis=1)

    fields = [
        jnp.concatenate([air_mass[None, l], tracer_mass[:, l]], axis=0) for l in range(levels)
    ]
    for step in range(ITERS):
        held = [[f] for f in fields]
        stride = 4
        while stride < count:
            for l in range(levels):
                held[l] = held[l] + [exchange(x, stride) for x in held[l]]
            stride *= 2
        mine, theirs = [], []
        for l in range(levels):
            other = [exchange(x, 1) for x in held[l]]
            kept, sent = cut_windows(held[l], other, plan[l])
            mine.append(kept)
            theirs.append(exchange(sent, 2))
        fields = stencils(mine, theirs, frac, courant, width, step)
    result = jnp.stack(fields, axis=1)
    return (result[0], result[1:])


def solution(mesh):
    return jax.shard_map(
        local,
        mesh=mesh,
        in_specs=(
            P(None, "lat", "lon"),
            P(None, None, "lat", "lon"),
            P(None, "lat", "lon"),
            P(None, "lat", "lon"),
            P(None, "lat"),
        ),
        out_specs=(P(None, "lat", "lon"), P(None, None, "lat", "lon")),
        check_vma=False,
    )
```

```python
import functools

import jax
import jax.numpy as jnp
from jax import lax
from jax.experimental import pallas as pl
from jax.experimental.pallas import tpu as pltpu
from jax.sharding import PartitionSpec as P

ITERS = 2
HALO = 3
LANES = 128


def round_up(value, unit=LANES):
    return -(-value // unit) * unit


def exchange(array, stride):
    count = lax.axis_size("lon")
    return lax.ppermute(array, "lon", [(i, i ^ stride) for i in range(count)])


def lat_halos(block, dim):
    count = lax.axis_size("lat")
    forward = [(i, i + 1) for i in range(count - 1)]
    backward = [(b, a) for a, b in forward]
    size = block.shape[dim]
    south = lax.ppermute(lax.slice_in_dim(block, size - HALO, size, axis=dim), "lat", forward)
    north = lax.ppermute(lax.slice_in_dim(block, 0, HALO, axis=dim), "lat", backward)
    return south, north


def right_amount(centre, left_edge, right_edge, fraction):
    slope = right_edge - left_edge
    curve = 6.0 * centre - 3.0 * (left_edge + right_edge)
    return fraction * (
        right_edge - 0.5 * fraction * (slope - (1.0 - fraction * (2.0 / 3.0)) * curve)
    )


def window_kernel(held, lead, width, plan, *refs):
    own = refs[:held]
    other = refs[held : 2 * held]
    mine, theirs, joined = refs[2 * held :]
    comps, band, _ = mine.shape
    out_width = mine.shape[2]

    def fill(low, high):
        for t in range(held):
            joined[t, :, :, lead : lead + width] = low[t][...]
            joined[t, :, :, lead + width : lead + 2 * width] = high[t][...]

    core = plan[0, 0]

    @pl.when(core == 0)
    def _():
        fill(own, other)

    @pl.when(core != 0)
    def _():
        fill(other, own)

    lane = lax.broadcasted_iota(jnp.int32, (comps, 1, LANES), 2)
    for target, out in ((1, mine), (3, theirs)):
        for j in range(band):
            slot = plan[target, j]
            first = plan[target + 1, j]
            begin = lead + jnp.maximum(first, -lead)
            tile = begin // LANES
            rest = begin - tile * LANES
            back = jnp.where(rest == 0, 0, LANES - rest)

            def piece(m):
                values = joined[slot, :, j : j + 1, pl.ds(pl.multiple_of((tile + m) * LANES, LANES), LANES)]
                return pltpu.roll(values, back, 2)

            now = piece(0)
            for m in range(out_width // LANES):
                later = piece(m + 1)
                values = jnp.where(lane < LANES - rest, now, later)
                place = lane + (first + m * LANES)
                inside = (place >= 0) & (place < 2 * width)
                out[:, j : j + 1, m * LANES : (m + 1) * LANES] = jnp.where(inside, values, 0.0)
                now = later


def cut_windows(own, other, plan):
    held = len(own)
    comps, band, width = own[0].shape
    out_width = round_up(width + 2 * HALO)
    lead = out_width
    total = round_up(lead + 2 * width) + out_width + 2 * LANES
    shape = jax.ShapeDtypeStruct((comps, band, out_width), jnp.float32)
    return pl.pallas_call(
        functools.partial(window_kernel, held, lead, width),
        out_shape=(shape, shape),
        in_specs=[pl.BlockSpec(memory_space=pltpu.SMEM)]
        + [pl.BlockSpec(memory_space=pltpu.VMEM)] * (2 * held),
        out_specs=(pl.BlockSpec(memory_space=pltpu.VMEM),) * 2,
        scratch_shapes=[pltpu.VMEM((held, comps, band, total), jnp.float32)],
        compiler_params=pltpu.CompilerParams(vmem_limit_bytes=32 * 1024 * 1024),
        cost_estimate=pl.CostEstimate(flops=2_000_000, bytes_accessed=2_000_000, transcendentals=0),
        name="cut_windows",
    )(plan, *own, *other)


def stencil_kernel(levels, rows, *refs):
    mine = refs[:levels]
    theirs = refs[levels : 2 * levels]
    frac, courant = refs[2 * levels : 2 * levels + 2]
    out = refs[2 * levels + 2 : 3 * levels + 2]
    to_north, to_south, south, north, send_sem, recv_sem = refs[3 * levels + 2 :]
    comps, band, width = out[0].shape
    full = mine[0].shape[2]
    count = lax.axis_size("lat")
    me = lax.axis_index("lat")
    has_south = me > 0
    has_north = me < count - 1
    used = comps * HALO

    barrier = pltpu.get_barrier_semaphore()

    def greet(step):
        pl.semaphore_signal(
            barrier, inc=1, device_id={"lat": me + step}, device_id_type=pl.DeviceIdType.MESH
        )

    pl.when(has_south)(lambda: greet(-1))
    pl.when(has_north)(lambda: greet(1))

    def northward_copy(l):
        return pltpu.make_async_remote_copy(
            src_ref=to_north.at[l], dst_ref=south.at[l],
            send_sem=send_sem.at[0, l], recv_sem=recv_sem.at[0, l],
            device_id={"lat": me + 1}, device_id_type=pl.DeviceIdType.MESH,
        )

    def southward_copy(l):
        return pltpu.make_async_remote_copy(
            src_ref=to_south.at[l], dst_ref=north.at[l],
            send_sem=send_sem.at[1, l], recv_sem=recv_sem.at[1, l],
            device_id={"lat": me - 1}, device_id_type=pl.DeviceIdType.MESH,
        )

    @pl.when(me == 0)
    def _():
        south[...] = jnp.zeros_like(south)

    @pl.when(me == count - 1)
    def _():
        north[...] = jnp.zeros_like(north)

    for l in range(levels):
        fraction = frac[l]
        for c in range(comps):
            w = mine[l][c] + theirs[l][c]
            w_1 = pltpu.roll(w, 1, 1)
            w_2 = pltpu.roll(w, 2, 1)
            w1 = pltpu.roll(w, full - 1, 1)
            face = (7.0 * (w_1 + w) - (w_2 + w1)) * (1.0 / 12.0)
            flux = right_amount(w_1, pltpu.roll(face, 1, 1), face, fraction)
            new = w + flux - pltpu.roll(flux, full - 1, 1)
            new = pltpu.roll(new, full - HALO, 1)[:, :width]
            out[l][c] = new
            to_north[l, c * HALO : (c + 1) * HALO] = new[band - HALO :]
            to_south[l, c * HALO : (c + 1) * HALO] = new[:HALO]
        if rows > used:
            pad = jnp.zeros((rows - used, width), jnp.float32)
            to_north[l, used:rows] = pad
            to_south[l, used:rows] = pad
        if l == 0:
            peers = has_south.astype(jnp.int32) + has_north.astype(jnp.int32)
            pl.semaphore_wait(barrier, peers)
        pl.when(has_north)(lambda l=l: northward_copy(l).start())
        pl.when(has_south)(lambda l=l: southward_copy(l).start())

    step = 2 * LANES
    for l in range(levels):
        pl.when(has_south)(lambda l=l: northward_copy(l).wait_recv())
        pl.when(has_north)(lambda l=l: southward_copy(l).wait_recv())
        for at in range(0, width, step):
            cols = slice(at, min(at + step, width))
            g = courant[l, HALO : HALO + band + 1, cols]
            half = 0.5 * g * g
            rest = 1.0 - jnp.abs(g) * (2.0 / 3.0)
            north_going = g > 0.0
            rest = jnp.where(north_going, rest, -rest)
            for c in range(comps):
                ends = slice(c * HALO, (c + 1) * HALO)
                padded = jnp.concatenate(
                    [south[l, ends, cols], out[l][c, :, cols], north[l, ends, cols]], axis=0
                )
                faces = (
                    7.0 * (padded[1:-2] + padded[2:-1]) - (padded[:-3] + padded[3:])
                ) * (1.0 / 12.0)
                slope = faces[1:] - faces[:-1]
                curve = 6.0 * padded[2 : band + 4] - 3.0 * (faces[1:] + faces[:-1])
                slope = jnp.where(north_going, slope[:-1], slope[1:])
                curve = jnp.where(north_going, curve[:-1], curve[1:])
                flux = g * faces[1 : band + 2] - half * (slope - rest * curve)
                out[l][c, :, cols] = padded[3 : band + 3] + flux[:band] - flux[1:]

    for l in range(levels):
        pl.when(has_north)(lambda l=l: northward_copy(l).wait_send())
        pl.when(has_south)(lambda l=l: southward_copy(l).wait_send())


def stencils(mine, theirs, frac, courant, width, step):
    levels = len(mine)
    comps, band, _ = mine[0].shape
    rows = round_up(comps * HALO, 8)
    shape = jax.ShapeDtypeStruct((comps, band, width), jnp.float32)
    vmem = pl.BlockSpec(memory_space=pltpu.VMEM)
    halo = pltpu.VMEM((levels, rows, width), jnp.float32)
    return pl.pallas_call(
        functools.partial(stencil_kernel, levels, rows),
        out_shape=(shape,) * levels,
        in_specs=[vmem] * (2 * levels + 2),
        out_specs=(vmem,) * levels,
        scratch_shapes=[
            halo, halo, halo, halo,
            pltpu.SemaphoreType.DMA((2, levels)),
            pltpu.SemaphoreType.DMA((2, levels)),
        ],
        compiler_params=pltpu.CompilerParams(
            vmem_limit_bytes=32 * 1024 * 1024, collective_id=step, has_side_effects=True
        ),
        cost_estimate=pl.CostEstimate(flops=20_000_000, bytes_accessed=5_000_000, transcendentals=0),
        name="stencils",
    )(*mine, *theirs, frac, courant)


def make_plan(shift, width, count, me):
    full = width * count
    parity = me // 2 % 2

    def towards(device):
        begin = jnp.mod(device * width - HALO - shift, full)
        pair = begin // (2 * width)
        offset = begin - pair * (2 * width)
        here = pair % 2 == parity
        chosen = jnp.where(here, pair, (pair + 1) % (count // 2))
        slot = (chosen // 2) ^ (me // 4)
        return [slot, jnp.where(here, offset, offset - 2 * width)]

    core = jnp.broadcast_to(me % 2, shift.shape)
    rows = [core] + towards(me) + towards(me ^ 2)
    return jnp.stack(rows, axis=1).astype(jnp.int32)


def local(air_mass, tracer_mass, zonal_frac, merid_courant, zonal_shift):
    levels, band, width = air_mass.shape
    count = lax.axis_size("lon")
    me = lax.axis_index("lon")
    global_row = lax.axis_index("lat") * band + jnp.arange(band, dtype=jnp.int32)
    courant = jnp.where(
        global_row[None, :, None] == 0, jnp.zeros_like(merid_courant), merid_courant
    )
    plan = make_plan(zonal_shift, width, count, me)

    ring = [(i, (i + 1) % count) for i in range(count)]
    west = lax.ppermute(zonal_frac[..., width - HALO :], "lon", ring)
    east = lax.ppermute(zonal_frac[..., :HALO], "lon", [(b, a) for a, b in ring])
    out_width = round_up(width + 2 * HALO)
    fill = jnp.zeros((levels, band, out_width - width - 2 * HALO), jnp.float32)
    frac = jnp.concatenate([west, zonal_frac, east, fill], axis=2)
    south, north = lat_halos(courant, 1)
    courant = jnp.concatenate([south, courant, north], axis=1)

    fields = [
        jnp.concatenate([air_mass[None, l], tracer_mass[:, l]], axis=0) for l in range(levels)
    ]
    def finish(group, call, held):
        mine, theirs = [], []
        for l in group:
            other = [exchange(x, 1) for x in held[l]]
            kept, sent = cut_windows(held[l], other, plan[l])
            mine.append(kept)
            theirs.append(exchange(sent, 2))
        rows = slice(group[0], group[-1] + 1)
        done = stencils(mine, theirs, frac[rows], courant[rows], width, call)
        for l, value in zip(group, done):
            fields[l] = value

    groups = [range(0, levels // 2), range(levels // 2, levels)]
    arrived = None
    for step in range(ITERS):
        for g, group in enumerate(groups):
            held = {l: [fields[l]] for l in group}
            if arrived is not None:
                arrived, held = lax.optimization_barrier((arrived, held))
                for l in previous:
                    waiting[l] = arrived[l]
            stride = 4
            while stride < count:
                for l in group:
                    held[l] = held[l] + [exchange(x, stride) for x in held[l]]
                stride *= 2
            if arrived is not None:
                finish(previous, previous_id, waiting)
            previous, previous_id = group, step * len(groups) + g
            waiting = dict(held)
            arrived = dict(held)
    finish(previous, previous_id, waiting)
    result = jnp.stack(fields, axis=1)
    return (result[0], result[1:])


def solution(mesh):
    return jax.shard_map(
        local,
        mesh=mesh,
        in_specs=(
            P(None, "lat", "lon"),
            P(None, None, "lat", "lon"),
            P(None, "lat", "lon"),
            P(None, "lat", "lon"),
            P(None, "lat"),
        ),
        out_specs=(P(None, "lat", "lon"), P(None, None, "lat", "lon")),
        check_vma=False,
    )
```
